32 devices in a mesh: dp: 8 (over z, core), tensor: 4 (over y, x).
Axes of the slice: x: 2, y: 2, z: 4, core: 2. Of those that a mesh axis runs over, the one named last changes fastest.
Arguments:
- tokens: bfloat16 [6144, 1024], P('dp'), may hold values from -72 to 72
- w_qkv: float32 [1024, 3072], P(('dp', 'tensor')), may hold values from -0.1875 to 0.1875
- w_out: float32 [1024, 1024], P(None, ('dp', 'tensor')), may hold values from -0.1875 to 0.1875
- w_up: float32 [1024, 4096], P(('dp', 'tensor')), may hold values from -0.1875 to 0.1875
- w_down: float32 [4096, 1024], P(None, ('dp', 'tensor')), may hold values from -0.09375 to 0.09375
- slot_request: int32 [48, 128], replicated, may hold values from -1 to 3, as said below
Outputs:
- encoded: bfloat16 [6144, 1024], P('dp')
The draws below stay inside these ranges and needn't reach their ends.
Inputs may be any that keep to these rules, and one draw needn't show every extreme that they name: `slot_request`: requests are numbered 0 to 3, all present; each request holds 1 to 24 pages and one holds exactly 24; each request's pages are full except its last page, whose empty slots are its final ones; pages may sit in any slot of the table.
All inputs are finite; a program needn't handle non-finite values.
Results may differ from the reference program's by a relative error of at most 0.025.
The reference program's roundings to bfloat16 on the way (of `qkv`, `probs`, `attn`, `first` and `inner`) count: a program that leaves them out, or rounds other values in their place, can miss the bound.
Values may be sent and summed in bfloat16 or wider, within the bound.
A program may use at most 128 MiB of HBM per device.

```python
import math
import jax
import jax.numpy as jnp
from jax import lax

D = 1024
H = 16
FF = 4096
PAGE = 128
REQS = 4
PAGES = 48
MAX_PAGES = 24
TOKENS = 6144


def draw_tokens(key, part):
    base_key = jax.random.fold_in(jax.random.fold_in(key, 11), 0)
    values = jnp.clip(jax.random.normal(base_key, (TOKENS, D), jnp.float32), -6.0, 6.0)
    return values.astype(jnp.bfloat16)


def draw_slot_request(key, part):
    order_key, weight_key, tie_key, place_key, fill_key = jax.random.split(jax.random.fold_in(key, 23), 5)
    others = REQS - 1
    extra_pips = MAX_PAGES - 1
    extra = PAGES - MAX_PAGES - others
    base = jax.random.randint(weight_key, (others,), 0, 128)
    heft = base * base // 64
    section = jnp.arange(extra_pips, dtype=jnp.int32)
    ties = jax.random.permutation(tie_key, others * extra_pips).reshape(others, extra_pips)
    score = ((heft[:, None] - 24 * section[None, :]) * 4096 + ties).reshape(-1)
    ranked = jnp.argsort(jnp.argsort(-score))
    chosen = (ranked < extra).astype(jnp.int32).reshape(others, extra_pips)
    rest = 1 + jnp.sum(chosen, axis=1)
    lengths = jnp.concatenate([jnp.full((1,), MAX_PAGES, jnp.int32), rest.astype(jnp.int32)])
    lengths = lengths[jax.random.permutation(place_key, REQS)]
    ends = jnp.cumsum(lengths).astype(jnp.int32)
    page = jnp.arange(PAGES, dtype=jnp.int32)
    request = jnp.sum((page[:, None] >= ends[None, :]).astype(jnp.int32), axis=1)
    is_last = page == ends[request] - 1
    fills = jax.random.randint(fill_key, (REQS,), 1, PAGE)
    position = jnp.arange(PAGE, dtype=jnp.int32)
    live = jnp.logical_or(jnp.logical_not(is_last)[:, None], position[None, :] < fills[request][:, None])
    logical = jnp.where(live, request[:, None], -1).astype(jnp.int32)
    order = jax.random.permutation(order_key, PAGES)
    return jnp.zeros((PAGES, PAGE), jnp.int32).at[order].set(logical)


def level_of(stream_key, dims, cuts, smallest, top_value):
    level, own = 1.0, jax.random.fold_in(stream_key, 6)
    for axis_at, blocks in cuts:
        heights = jnp.exp(jax.random.uniform(jax.random.fold_in(own, axis_at), (blocks,), jnp.float32, smallest / len(cuts), top_value / len(cuts)))
        level = level * jnp.repeat(heights, dims[axis_at] // blocks).reshape([-1 if axis == axis_at else 1 for axis in range(len(dims))])
    return level


def gaussian(stream_key, extent, scale, bound, cuts=(), kind=jnp.bfloat16):
    values = jax.random.normal(stream_key, extent, jnp.float32) * scale
    if len(cuts) > 0:
        values = level_of(stream_key, extent, cuts, -0.22, 0.18) * values
    return jnp.clip(values, min=-bound, max=bound).astype(kind)


def setup_inputs(seed: int = 0) -> dict:
    key_of = jax.random.split(jax.random.key(seed), 7)
    tokens = draw_tokens(jax.random.fold_in(key_of[6], 71), 0)
    w_qkv = gaussian(key_of[1], (D, 3 * D), D ** -0.5, 0.1875, ((0, 32),), jnp.float32)
    w_out = gaussian(key_of[2], (D, D), D ** -0.5, 0.1875, ((1, 32),), jnp.float32)
    w_up = gaussian(key_of[3], (D, FF), D ** -0.5, 0.1875, ((0, 32),), jnp.float32)
    w_down = gaussian(key_of[4], (FF, D), FF ** -0.5, 0.09375, ((1, 32),), jnp.float32)
    slot_request = draw_slot_request(jax.random.fold_in(key_of[6], 71), 0)
    return dict(tokens=tokens, w_qkv=w_qkv, w_out=w_out, w_up=w_up, w_down=w_down, slot_request=slot_request)


def layer_norm(value):
    mean = lax.optimization_barrier(jnp.mean(value, axis=-1, keepdims=True))
    centred = value - mean
    spread = lax.optimization_barrier(jnp.mean(centred * centred, axis=-1, keepdims=True))
    return centred * lax.rsqrt(spread + 1e-05)

def reference(tokens, w_qkv, w_out, w_up, w_down, slot_request):
    qkv_w = w_qkv.astype(jnp.bfloat16)
    out_w = w_out.astype(jnp.bfloat16)
    up_w = w_up.astype(jnp.bfloat16)
    down_w = w_down.astype(jnp.bfloat16)
    count = tokens.shape[0]
    head_size = D // H
    qkv = jnp.dot(tokens, qkv_w, preferred_element_type=jnp.float32).astype(jnp.bfloat16)
    qkv = qkv.reshape(count, H, 3, head_size)
    queries = qkv[:, :, 0, :]
    key_rows = qkv[:, :, 1, :].astype(jnp.float32)
    value_rows = qkv[:, :, 2, :].astype(jnp.float32)
    slot_ids = slot_request.reshape(-1)
    block = math.gcd(count, 256)
    query_blocks = queries.reshape(count // block, block, H, head_size)
    id_blocks = slot_ids.reshape(count // block, block)
    scale = 1.0 / math.sqrt(head_size)

    def one_block(args):
        query_block, id_block = args
        scores = jnp.einsum('qhd,khd->hqk', query_block.astype(jnp.float32), key_rows) * scale
        allowed = (id_block[:, None] == slot_ids[None, :])[None]
        masked = jnp.where(allowed, scores, -1e+30)
        top = lax.optimization_barrier(jnp.max(masked, axis=-1, keepdims=True))
        weights = jnp.where(allowed, jnp.exp(masked - top), 0.0)
        probs = (weights / lax.optimization_barrier(jnp.sum(weights, axis=-1, keepdims=True))).astype(jnp.bfloat16)
        mixed = jnp.einsum('hqk,khd->qhd', probs.astype(jnp.float32), value_rows)
        return mixed.astype(jnp.bfloat16)
    attn = lax.map(one_block, (query_blocks, id_blocks)).reshape(count, D)
    proj = jnp.dot(attn, out_w, preferred_element_type=jnp.float32)
    first = layer_norm(tokens.astype(jnp.float32) + proj).astype(jnp.bfloat16)
    inner = jax.nn.gelu(jnp.dot(first, up_w, preferred_element_type=jnp.float32), approximate=False).astype(jnp.bfloat16)
    ffn = jnp.dot(inner, down_w, preferred_element_type=jnp.float32)
    live = (slot_ids >= 0).astype(jnp.float32)[:, None]
    encoded = layer_norm(first.astype(jnp.float32) + ffn) * live
    return encoded.astype(jnp.bfloat16)
```

```python
import functools

import jax
import jax.numpy as jnp
from jax import lax
from jax.experimental import pallas as pl
from jax.experimental.pallas import tpu as pltpu
from jax.sharding import PartitionSpec as P

HEAD = 64
MESH = pl.DeviceIdType.MESH
GROUP = 4
BF = jnp.bfloat16
F32 = jnp.float32


def greet(targets):
    barrier = pltpu.get_barrier_semaphore()
    for cond, dev in targets:
        if cond is None:
            pl.semaphore_signal(barrier, inc=1, device_id=dev, device_id_type=MESH)
        else:

            @pl.when(cond)
            def _(dev=dev):
                pl.semaphore_signal(barrier, inc=1, device_id=dev, device_id_type=MESH)

    count = sum(1 if cond is None else jnp.where(cond, 1, 0) for cond, _ in targets)
    pl.semaphore_wait(barrier, count)


def exchange_kernel(groups, x_ref, out_ref, send_sem, recv_sem, local_sem):
    dp = lax.axis_index("dp")
    me = lax.axis_index("tensor")
    greet([(None, (dp, lax.rem(me + k, groups))) for k in range(1, groups)])
    local = pltpu.make_async_copy(x_ref.at[me], out_ref.at[me], local_sem)
    local.start()
    sends = []
    for k in range(1, groups):
        peer = lax.rem(me + k, groups)
        copy = pltpu.make_async_remote_copy(
            x_ref.at[peer], out_ref.at[me], send_sem.at[k], recv_sem.at[k],
            device_id=(dp, peer), device_id_type=MESH,
        )
        copy.start()
        sends.append(copy)
    for copy in sends:
        copy.wait()
    local.wait()


def exchange(x, groups, cid):
    return pl.pallas_call(
        functools.partial(exchange_kernel, groups),
        out_shape=jax.ShapeDtypeStruct(x.shape, x.dtype),
        in_specs=[pl.BlockSpec(memory_space=pl.ANY)],
        out_specs=pl.BlockSpec(memory_space=pl.ANY),
        scratch_shapes=[
            pltpu.SemaphoreType.DMA((groups,)),
            pltpu.SemaphoreType.DMA((groups,)),
            pltpu.SemaphoreType.DMA,
        ],
        compiler_params=pltpu.CompilerParams(collective_id=cid, has_side_effects=True),
        name="exchange",
    )(x)


def gather_kernel(chips, x_ref, out_ref, right_sem, left_sem, core_sem, recv_sem, local_sem):
    dp = lax.axis_index("dp")
    tensor = lax.axis_index("tensor")
    chip, core = dp // 2, lax.rem(dp, 2)
    other = 1 - core
    partner = (2 * chip + other, tensor)
    has_right, has_left = chip + 1 < chips, chip > 0
    right = (2 * jnp.minimum(chip + 1, chips - 1) + core, tensor)
    left = (2 * jnp.maximum(chip - 1, 0) + core, tensor)
    greet([(None, partner), (has_right, right), (has_left, left)])
    local = pltpu.make_async_copy(x_ref, out_ref.at[dp], local_sem)
    local.start()

    def copy_of(source, block, send, device):
        return pltpu.make_async_remote_copy(
            source, out_ref.at[block], send, recv_sem.at[block],
            device_id=device, device_id_type=MESH,
        )

    @pl.when(has_right)
    def _():
        copy_of(x_ref, dp, right_sem.at[0], right).start()

    @pl.when(has_left)
    def _():
        copy_of(x_ref, dp, left_sem.at[0], left).start()

    copy_of(x_ref, dp, core_sem.at[chip], partner).start()
    for s in range(1, chips):
        for away, has_next, sems, following in (
            (chip - s, has_right, right_sem, right),
            (chip + s, has_left, left_sem, left),
        ):

            @pl.when(jnp.logical_and(away >= 0, away < chips))
            def _(away=away, has_next=has_next, sems=sems, following=following, s=s):
                block = 2 * away + core
                copy_of(out_ref.at[block], block, core_sem.at[away], partner).wait_recv()

                @pl.when(has_next)
                def _():
                    copy_of(out_ref.at[block], block, sems.at[s], following).start()

                copy_of(out_ref.at[block], block, core_sem.at[away], partner).start()

    for away in range(chips):
        block = 2 * away + other
        copy_of(x_ref, block, core_sem.at[away], partner).wait_recv()
        copy_of(x_ref, block, core_sem.at[away], partner).wait_send()
    for s in range(chips):

        @pl.when(jnp.logical_and(has_right, chip - s >= 0))
        def _(s=s):
            copy_of(x_ref, dp, right_sem.at[s], right).wait_send()

        @pl.when(jnp.logical_and(has_left, chip + s < chips))
        def _(s=s):
            copy_of(x_ref, dp, left_sem.at[s], left).wait_send()

    local.wait()


def gather_dp(x, cid):
    n = lax.axis_size("dp")
    chips = n // 2
    return pl.pallas_call(
        functools.partial(gather_kernel, chips),
        out_shape=jax.ShapeDtypeStruct((n,) + x.shape, x.dtype),
        in_specs=[pl.BlockSpec(memory_space=pl.ANY)],
        out_specs=pl.BlockSpec(memory_space=pl.ANY),
        scratch_shapes=[
            pltpu.SemaphoreType.DMA((chips,)),
            pltpu.SemaphoreType.DMA((chips,)),
            pltpu.SemaphoreType.DMA((chips,)),
            pltpu.SemaphoreType.DMA((n,)),
            pltpu.SemaphoreType.DMA,
        ],
        compiler_params=pltpu.CompilerParams(collective_id=cid, has_side_effects=True),
        cost_estimate=pl.CostEstimate(
            flops=0, bytes_accessed=n * x.size * 4, transcendentals=0
        ),
        name="gather_dp",
    )(x)


def attend_kernel(heads, page, pages_ref, count_ref, q_ref, kv_ref, qid_ref, kid_ref, out_ref, qbd):
    width = heads * HEAD
    step = pl.program_id(0)
    col = lax.broadcasted_iota(jnp.int32, (page, width), 1) // HEAD
    q = q_ref[...] * jnp.asarray(0.125, BF)
    for h in range(heads):
        qbd[h * page : (h + 1) * page, :] = jnp.where(col == h, q, jnp.zeros_like(q))
    own = jnp.concatenate([qid_ref[...]] * heads, axis=0)
    rows = heads * page
    count = count_ref[step]

    def body(i, carry):
        top, total, acc = carry
        keys, values, ids = [], [], []
        for g in range(GROUP):
            at = i * GROUP + g
            p = pages_ref[step, at]
            block = kv_ref[pl.ds(pl.multiple_of(p * page, page), page), :]
            keys.append(block[:, :width])
            values.append(block[:, width:])
            ids.append(jnp.where(at < count, kid_ref[pl.ds(p, 1), :], -2))
        key = jnp.concatenate(keys, axis=0)
        value = jnp.concatenate(values, axis=0)
        kid = jnp.concatenate(ids, axis=1)
        s = lax.dot_general(qbd[...], key, (((1,), (1,)), ((), ())), preferred_element_type=F32)
        s = jnp.where(own == kid, s, -1e30)
        new_top = jnp.maximum(top, jnp.max(s, axis=1, keepdims=True))
        w = jnp.exp(s - new_top)
        alpha = jnp.exp(top - new_top)
        total = total * alpha + jnp.sum(w, axis=1, keepdims=True)
        acc = acc * alpha + jnp.dot(w.astype(BF), value, preferred_element_type=F32)
        return new_top, total, acc

    init = (
        jnp.full((rows, 1), -1e29, F32),
        jnp.zeros((rows, 1), F32),
        jnp.zeros((rows, width), F32),
    )
    _, total, acc = lax.fori_loop(0, (count + GROUP - 1) // GROUP, body, init)
    acc = acc / total
    result = jnp.zeros((page, width), F32)
    for h in range(heads):
        result = result + jnp.where(col == h, acc[h * page : (h + 1) * page, :], 0.0)
    out_ref[...] = result.astype(BF)


def attend(q, kv, slots, dp):
    rows, width = q.shape
    total_pages, page = slots.shape
    heads = width // HEAD
    own_pages = rows // page
    requests = jnp.arange(-1, 4, dtype=jnp.int32)
    holds = jnp.any(slots[:, :, None] == requests[None, None, :], axis=1)
    own_holds = lax.dynamic_slice_in_dim(holds, dp * own_pages, own_pages, 0)
    need = jnp.any(own_holds[:, None, :] & holds[None, :, :], axis=-1)
    need_int = need.astype(jnp.int32)
    index = jnp.arange(total_pages, dtype=jnp.int32)
    before = (index[:, None] > index[None, :]).astype(jnp.int32)
    place = jnp.sum(need_int[:, None, :] * before[None], axis=-1)
    hit = need[:, :, None] & (place[:, :, None] == index[None, None, :])
    lists = jnp.sum(jnp.where(hit, index[None, :, None], 0), axis=1).astype(jnp.int32)
    lists = jnp.pad(lists, ((0, 0), (0, GROUP)))
    counts = jnp.sum(need_int, axis=1).astype(jnp.int32)
    own_ids = lax.dynamic_slice_in_dim(slots.reshape(-1), dp * rows, rows, 0)[:, None]
    return pl.pallas_call(
        functools.partial(attend_kernel, heads, page),
        out_shape=jax.ShapeDtypeStruct(q.shape, BF),
        grid_spec=pltpu.PrefetchScalarGridSpec(
            num_scalar_prefetch=2,
            grid=(own_pages,),
            in_specs=[
                pl.BlockSpec((page, width), lambda i, *_: (i, 0)),
                pl.BlockSpec(kv.shape, lambda i, *_: (0, 0)),
                pl.BlockSpec((page, 1), lambda i, *_: (i, 0)),
                pl.BlockSpec(slots.shape, lambda i, *_: (0, 0)),
            ],
            out_specs=pl.BlockSpec((page, width), lambda i, *_: (i, 0)),
            scratch_shapes=[pltpu.VMEM((heads * page, width), BF)],
        ),
        compiler_params=pltpu.CompilerParams(vmem_limit_bytes=40 * 2**20),
        cost_estimate=pl.CostEstimate(
            flops=rows * kv.shape[0] * 256 * 4 * 2, bytes_accessed=2 * kv.size,
            transcendentals=rows * kv.shape[0] * heads // 2,
        ),
        name="attend",
    )(lists, counts, q, kv, own_ids, slots)


def norm(value):
    mean = jnp.mean(value, axis=-1, keepdims=True)
    centred = value - mean
    spread = jnp.mean(centred * centred, axis=-1, keepdims=True)
    return centred * lax.rsqrt(spread + 1e-05)


def tail_kernel(
    groups, attn_ref, tok_ref, up_ref, down_ref, wout_ref, live_ref, out_ref,
    heads_buf, part_out, part_in, result,
    attn_send, attn_recv, part_send, part_recv, out_send, out_recv, local_sem,
):
    dp = lax.axis_index("dp")
    me = lax.axis_index("tensor")
    rows = attn_ref.shape[0] // groups
    width = attn_ref.shape[1]

    def span(j):
        return pl.ds(pl.multiple_of(j * rows, rows), rows)

    greet([(None, (dp, lax.rem(me + k, groups))) for k in range(1, groups)])
    own = pltpu.make_async_copy(attn_ref, heads_buf.at[me], local_sem)
    own.start()

    def attn_copy(k, i):
        peer = lax.rem(me + k, groups)
        at = span(lax.rem(peer + 1 + i, groups))
        return pltpu.make_async_remote_copy(
            attn_ref.at[at], heads_buf.at[me, at], attn_send.at[k, i], attn_recv.at[k, i],
            device_id=(dp, peer), device_id_type=MESH,
        )

    def part_copy(i):
        peer = lax.rem(me + 1 + i, groups)
        return pltpu.make_async_remote_copy(
            part_out.at[i], part_in.at[i], part_send.at[i], part_recv.at[i],
            device_id=(dp, peer), device_id_type=MESH,
        )

    def out_copy(k):
        peer = lax.rem(me + k, groups)
        return pltpu.make_async_remote_copy(
            result, out_ref.at[span(me)], out_send.at[k], out_recv.at[k],
            device_id=(dp, peer), device_id_type=MESH,
        )

    for i in range(groups):
        for k in range(1, groups):
            attn_copy(k, i).start()
    own.wait()
    for i in range(groups):
        for k in range(1, groups):
            attn_copy(k, i).wait_recv()
        at = span(lax.rem(me + 1 + i, groups))
        attn = jnp.concatenate([heads_buf[t, at, :] for t in range(groups)], axis=1)
        proj = lax.dot_general(
            attn, wout_ref[...], (((1,), (1,)), ((), ())), preferred_element_type=F32
        )
        first = norm(tok_ref[at, :].astype(F32) + proj).astype(BF)
        hidden = jnp.dot(first, up_ref[...], preferred_element_type=F32)
        inner = (0.5 * hidden * (1.0 + lax.erf(hidden * 0.7071067811865476))).astype(BF)
        part = lax.dot_general(
            inner, down_ref[...], (((1,), (1,)), ((), ())), preferred_element_type=F32
        )
        if i < groups - 1:
            part_out[i] = part.astype(BF)
            part_copy(i).start()
        else:
            total = part
            for n in range(groups - 1):
                part_copy(n).wait_recv()
                total = total + part_in[n].astype(F32)
            value = norm(first.astype(F32) + total) * live_ref[at, :]
            result[...] = value.astype(BF)
    final = pltpu.make_async_copy(result, out_ref.at[span(me)], local_sem)
    final.start()
    for k in range(1, groups):
        out_copy(k).start()
    for k in range(1, groups):
        out_copy(k).wait()
        for i in range(groups):
            attn_copy(k, i).wait_send()
    for n in range(groups - 1):
        part_copy(n).wait_send()
    final.wait()


def tail(attn, tokens, up, down, wout, live, groups, cid):
    rows, width = attn.shape
    wide = tokens.shape[1]
    share = rows // groups
    vmem = pl.BlockSpec(memory_space=pltpu.VMEM)
    return pl.pallas_call(
        functools.partial(tail_kernel, groups),
        out_shape=jax.ShapeDtypeStruct(tokens.shape, BF),
        in_specs=[vmem] * 6,
        out_specs=pl.BlockSpec(memory_space=pl.ANY),
        scratch_shapes=[
            pltpu.VMEM((groups, rows, width), BF),
            pltpu.VMEM((groups - 1, share, wide), BF),
            pltpu.VMEM((groups - 1, share, wide), BF),
            pltpu.VMEM((share, wide), BF),
            pltpu.SemaphoreType.DMA((groups, groups)),
            pltpu.SemaphoreType.DMA((groups, groups)),
            pltpu.SemaphoreType.DMA((groups,)),
            pltpu.SemaphoreType.DMA((groups,)),
            pltpu.SemaphoreType.DMA((groups,)),
            pltpu.SemaphoreType.DMA((groups,)),
            pltpu.SemaphoreType.DMA,
        ],
        compiler_params=pltpu.CompilerParams(
            collective_id=cid, has_side_effects=True, vmem_limit_bytes=48 * 2**20
        ),
        name="tail",
    )(attn, tokens, up, down, wout, live)


def shards(tokens, w_qkv, w_out, w_up, w_down, slot_request):
    groups = lax.axis_size("tensor")
    dp = lax.axis_index("dp")
    slab, wide = w_qkv.shape[0], tokens.shape[1]
    heads = wide // HEAD // groups
    width = heads * HEAD
    rows = tokens.shape[0]

    qkv_w = w_qkv.astype(BF).reshape(slab, groups, heads, 3, HEAD)
    qkv_w = jnp.transpose(qkv_w, (1, 0, 3, 2, 4)).reshape(groups, slab, 3 * width)
    up_w = jnp.transpose(w_up.astype(BF).reshape(slab, groups, -1), (1, 0, 2))
    down_w = jnp.transpose(w_down.astype(BF).reshape(groups, -1, slab), (0, 2, 1))
    out_w = jnp.broadcast_to(jnp.transpose(w_out.astype(BF))[None], (groups, slab, wide))
    packed = jnp.concatenate([qkv_w, up_w, down_w, out_w], axis=2)
    cut = 3 * width
    ff = up_w.shape[2]
    mine = exchange(packed, groups, 0).reshape(groups * slab, -1)
    rest = lax.all_gather(mine[:, cut:], "dp", axis=0, tiled=True)
    qkv_block = gather_dp(mine[:, :cut], 1).reshape(wide, cut)
    qkv = jnp.dot(tokens, qkv_block, preferred_element_type=F32).astype(BF)
    kv = gather_dp(qkv[:, width:], 2).reshape(-1, 2 * width)
    attn = attend(qkv[:, :width], kv, slot_request, dp)
    own_ids = lax.dynamic_slice_in_dim(slot_request.reshape(-1), dp * rows, rows, 0)
    live = (own_ids >= 0).astype(F32)[:, None]
    return tail(
        attn, tokens, rest[:, :ff], rest[:, ff : 2 * ff], rest[:, 2 * ff :], live, groups, 3
    )


def solution(mesh):
    in_specs = (
        P("dp", None),
        P(("dp", "tensor"), None),
        P(None, ("dp", "tensor")),
        P(("dp", "tensor"), None),
        P(None, ("dp", "tensor")),
        P(),
    )
    out_specs = P("dp", None)
    return jax.shard_map(shards, mesh=mesh, in_specs=in_specs, out_specs=out_specs, check_vma=False)
```

```python
import functools

import jax
import jax.numpy as jnp
from jax import lax
from jax.experimental import pallas as pl
from jax.experimental.pallas import tpu as pltpu
from jax.sharding import PartitionSpec as P

HEAD = 64
MESH = pl.DeviceIdType.MESH
GROUP = 4
BF = jnp.bfloat16
F32 = jnp.float32


def greet(targets):
    barrier = pltpu.get_barrier_semaphore()
    for cond, dev in targets:
        if cond is None:
            pl.semaphore_signal(barrier, inc=1, device_id=dev, device_id_type=MESH)
        else:

            @pl.when(cond)
            def _(dev=dev):
                pl.semaphore_signal(barrier, inc=1, device_id=dev, device_id_type=MESH)

    count = sum(1 if cond is None else jnp.where(cond, 1, 0) for cond, _ in targets)
    pl.semaphore_wait(barrier, count)


def exchange_kernel(groups, count, *refs):
    x_refs, out_refs = refs[:count], refs[count : 2 * count]
    send_sem, recv_sem, local_sem = refs[2 * count :]
    dp = lax.axis_index("dp")
    me = lax.axis_index("tensor")
    greet([(None, (dp, lax.rem(me + k, groups))) for k in range(1, groups)])
    sends = []
    for n in range(count):
        for k in range(1, groups):
            peer = lax.rem(me + k, groups)
            copy = pltpu.make_async_remote_copy(
                x_refs[n].at[peer], out_refs[n].at[me], send_sem.at[n, k], recv_sem.at[n, k],
                device_id=(dp, peer), device_id_type=MESH,
            )
            copy.start()
            sends.append(copy)
        local = pltpu.make_async_copy(x_refs[n].at[me], out_refs[n].at[me], local_sem.at[n])
        local.start()
        sends.append(local)
    for copy in sends:
        copy.wait()


def exchange(arrays, groups, cid):
    count = len(arrays)
    hbm = pl.BlockSpec(memory_space=pl.ANY)
    return pl.pallas_call(
        functools.partial(exchange_kernel, groups, count),
        out_shape=[jax.ShapeDtypeStruct(x.shape, x.dtype) for x in arrays],
        in_specs=[hbm] * count,
        out_specs=[hbm] * count,
        scratch_shapes=[
            pltpu.SemaphoreType.DMA((count, groups)),
            pltpu.SemaphoreType.DMA((count, groups)),
            pltpu.SemaphoreType.DMA((count,)),
        ],
        compiler_params=pltpu.CompilerParams(collective_id=cid, has_side_effects=True),
        name="exchange",
    )(*arrays)


def gather_kernel(chips, count, cols, groups, *refs):
    total = count + (1 if groups else 0)
    x_refs, out_refs = list(refs[:total]), refs[total : 2 * total]
    right_sem, left_sem, core_sem, recv_sem, local_sem, side_send, side_recv = refs[2 * total :]
    dp = lax.axis_index("dp")
    tensor = lax.axis_index("tensor")
    chip, core = dp // 2, lax.rem(dp, 2)
    other = 1 - core
    partner = (2 * chip + other, tensor)
    has_right, has_left = chip + 1 < chips, chip > 0
    right = (2 * jnp.minimum(chip + 1, chips - 1) + core, tensor)
    left = (2 * jnp.maximum(chip - 1, 0) + core, tensor)
    peers = [(dp, lax.rem(tensor + k, groups)) for k in range(1, groups)] if groups else []
    greet(
        [(None, partner), (has_right, right), (has_left, left)]
        + [(None, peer) for peer in peers]
    )
    if cols is not None:
        x_refs[0] = x_refs[0].at[:, cols[0] : cols[1]]

    def copy_of(n, source, block, send, device):
        return pltpu.make_async_remote_copy(
            source, out_refs[n].at[block], send, recv_sem.at[n, block],
            device_id=device, device_id_type=MESH,
        )

    for n in range(count):

        @pl.when(has_right)
        def _(n=n):
            copy_of(n, x_refs[n], dp, right_sem.at[n, 0], right).start()

        @pl.when(has_left)
        def _(n=n):
            copy_of(n, x_refs[n], dp, left_sem.at[n, 0], left).start()

        copy_of(n, x_refs[n], dp, core_sem.at[n, chip], partner).start()
    for n in range(count):
        pltpu.make_async_copy(x_refs[n], out_refs[n].at[dp], local_sem.at[n]).start()
    side = []
    for k, peer in enumerate(peers):
        side.append(
            pltpu.make_async_remote_copy(
                x_refs[count], out_refs[count].at[tensor], side_send.at[k], side_recv.at[k],
                device_id=peer, device_id_type=MESH,
            )
        )
    if groups:
        side.append(
            pltpu.make_async_copy(
                x_refs[count], out_refs[count].at[tensor], local_sem.at[count]
            )
        )
    for copy in side:
        copy.start()
    for s in range(1, chips):
        for n in range(count):
            for away, has_next, sems, following in (
                (chip - s, has_right, right_sem, right),
                (chip + s, has_left, left_sem, left),
            ):

                @pl.when(jnp.logical_and(away >= 0, away < chips))
                def _(n=n, away=away, has_next=has_next, sems=sems, following=following, s=s):
                    block = 2 * away + core
                    here = out_refs[n].at[block]
                    copy_of(n, here, block, core_sem.at[n, away], partner).wait_recv()

                    @pl.when(has_next)
                    def _():
                        copy_of(n, here, block, sems.at[n, s], following).start()

                    copy_of(n, here, block, core_sem.at[n, away], partner).start()

    for n in range(count):
        for away in range(chips):
            block = 2 * away + other
            copy_of(n, x_refs[n], block, core_sem.at[n, away], partner).wait()
        for s in range(chips):

            @pl.when(jnp.logical_and(has_right, chip - s >= 0))
            def _(n=n, s=s):
                copy_of(n, x_refs[n], dp, right_sem.at[n, s], right).wait_send()

            @pl.when(jnp.logical_and(has_left, chip + s < chips))
            def _(n=n, s=s):
                copy_of(n, x_refs[n], dp, left_sem.at[n, s], left).wait_send()

        pltpu.make_async_copy(x_refs[n], out_refs[n].at[dp], local_sem.at[n]).wait()
    for copy in side:
        copy.wait()


def gather_dp(arrays, cid, cols=None, side=None, groups=0):
    n = lax.axis_size("dp")
    chips = n // 2
    count = len(arrays)
    shapes = [x.shape for x in arrays]
    if cols is not None:
        shapes[0] = (shapes[0][0], cols[1] - cols[0])
    shapes = [(n,) + shape for shape in shapes]
    if side is not None:
        arrays = arrays + [side]
        shapes.append((groups,) + side.shape)
    hbm = pl.BlockSpec(memory_space=pl.ANY)
    return pl.pallas_call(
        functools.partial(gather_kernel, chips, count, cols, groups),
        out_shape=[jax.ShapeDtypeStruct(shape, BF) for shape in shapes],
        in_specs=[hbm] * len(shapes),
        out_specs=[hbm] * len(shapes),
        scratch_shapes=[
            pltpu.SemaphoreType.DMA((count, chips)),
            pltpu.SemaphoreType.DMA((count, chips)),
            pltpu.SemaphoreType.DMA((count, chips)),
            pltpu.SemaphoreType.DMA((count, n)),
            pltpu.SemaphoreType.DMA((count + 1,)),
            pltpu.SemaphoreType.DMA((max(groups, 1),)),
            pltpu.SemaphoreType.DMA((max(groups, 1),)),
        ],
        compiler_params=pltpu.CompilerParams(collective_id=cid, has_side_effects=True),
        cost_estimate=pl.CostEstimate(
            flops=0, bytes_accessed=n * arrays[0].size * 4, transcendentals=0
        ),
        name="gather_dp",
    )(*arrays)


def attend_kernel(heads, page, pages_ref, count_ref, q_ref, kv_ref, qid_ref, kid_ref, out_ref, qbd):
    width = heads * HEAD
    pair = 2 * HEAD
    step = pl.program_id(0)
    low = lax.broadcasted_iota(jnp.int32, (page, pair), 1) < HEAD
    q = q_ref[...] * jnp.asarray(0.125, BF)
    zero = jnp.zeros((page, pair), BF)
    for h in range(heads // 2):
        both = q[:, h * pair : (h + 1) * pair]
        qbd[h, :page, :] = jnp.where(low, both, zero)
        qbd[h, page:, :] = jnp.where(low, zero, both)
    own = jnp.concatenate([qid_ref[...]] * 2, axis=0)
    rows = 2 * page
    count = count_ref[step]

    def body(i, carry):
        blocks, ids = [], []
        for g in range(GROUP):
            at = i * GROUP + g
            p = pages_ref[step, at]
            blocks.append(kv_ref[pl.ds(pl.multiple_of(p * page, page), page), :])
            ids.append(jnp.where(at < count, kid_ref[pl.ds(p, 1), :], -2))
        block = jnp.concatenate(blocks, axis=0)
        kid = jnp.concatenate(ids, axis=1)
        allowed = own == kid
        after = []
        scores = [
            lax.dot_general(
                qbd[h], block[:, h * pair : (h + 1) * pair],
                (((1,), (1,)), ((), ())), preferred_element_type=F32,
            )
            for h in range(heads // 2)
        ]
        for h in range(heads // 2):
            top, total, acc = carry[h]
            value = block[:, width + h * pair : width + (h + 1) * pair]
            s = jnp.where(allowed, scores[h], -1e30)
            new_top = jnp.maximum(top, jnp.max(s, axis=1, keepdims=True))
            w = jnp.exp(s - new_top)
            alpha = jnp.exp(top - new_top)
            total = total * alpha + jnp.sum(w, axis=1, keepdims=True)
            acc = acc * alpha + jnp.dot(w.astype(BF), value, preferred_element_type=F32)
            after.append((new_top, total, acc))
        return tuple(after)

    init = (
        jnp.full((rows, 1), -1e29, F32),
        jnp.zeros((rows, 1), F32),
        jnp.zeros((rows, pair), F32),
    )
    final = lax.fori_loop(0, (count + GROUP - 1) // GROUP, body, (init,) * (heads // 2))
    for h in range(heads // 2):
        _, total, acc = final[h]
        acc = (acc / total).astype(BF)
        out_ref[:, h * pair : (h + 1) * pair] = jnp.where(low, acc[:page], acc[page:])


def attend(q, kv, slots, dp):
    rows, width = q.shape[0], kv.shape[1] // 2
    total_pages, page = slots.shape
    heads = width // HEAD
    own_pages = rows // page
    requests = jnp.arange(-1, 4, dtype=jnp.int32)
    holds = jnp.any(slots[:, :, None] == requests[None, None, :], axis=1)
    own_holds = lax.dynamic_slice_in_dim(holds, dp * own_pages, own_pages, 0)
    need = jnp.any(own_holds[:, None, :] & holds[None, :, :], axis=-1)
    need_int = need.astype(jnp.int32)
    index = jnp.arange(total_pages, dtype=jnp.int32)
    before = (index[:, None] > index[None, :]).astype(jnp.int32)
    place = jnp.sum(need_int[:, None, :] * before[None], axis=-1)
    hit = need[:, :, None] & (place[:, :, None] == index[None, None, :])
    lists = jnp.sum(jnp.where(hit, index[None, :, None], 0), axis=1).astype(jnp.int32)
    lists = jnp.pad(lists, ((0, 0), (0, GROUP)))
    counts = jnp.sum(need_int, axis=1).astype(jnp.int32)
    own_ids = lax.dynamic_slice_in_dim(slots.reshape(-1), dp * rows, rows, 0)[:, None]
    return pl.pallas_call(
        functools.partial(attend_kernel, heads, page),
        out_shape=jax.ShapeDtypeStruct((rows, width), BF),
        grid_spec=pltpu.PrefetchScalarGridSpec(
            num_scalar_prefetch=2,
            grid=(own_pages,),
            in_specs=[
                pl.BlockSpec((page, width), lambda i, *_: (i, 0)),
                pl.BlockSpec(kv.shape, lambda i, *_: (0, 0)),
                pl.BlockSpec((page, 1), lambda i, *_: (i, 0)),
                pl.BlockSpec(slots.shape, lambda i, *_: (0, 0)),
            ],
            out_specs=pl.BlockSpec((page, width), lambda i, *_: (i, 0)),
            scratch_shapes=[pltpu.VMEM((heads // 2, 2 * page, 2 * HEAD), BF)],
        ),
        compiler_params=pltpu.CompilerParams(vmem_limit_bytes=40 * 2**20),
        cost_estimate=pl.CostEstimate(
            flops=rows * kv.shape[0] * 256 * 4 * 2, bytes_accessed=2 * kv.size,
            transcendentals=rows * kv.shape[0] * heads // 2,
        ),
        name="attend",
    )(lists, counts, q, kv, own_ids, slots)


def norm(value):
    mean = jnp.mean(value, axis=-1, keepdims=True)
    centred = value - mean
    spread = jnp.mean(centred * centred, axis=-1, keepdims=True)
    return centred * lax.rsqrt(spread + 1e-05)


def tail_kernel(
    groups, attn_ref, tok_ref, ffw_ref, wout_ref, live_ref, out_ref,
    heads_buf, wout, part_out, part_in, result,
    attn_send, attn_recv, part_send, part_recv, out_send, out_recv, local_sem,
):
    dp = lax.axis_index("dp")
    me = lax.axis_index("tensor")
    rows = attn_ref.shape[0] // groups
    width = attn_ref.shape[1]
    ff = ffw_ref.shape[1] // 2

    def span(j):
        return pl.ds(pl.multiple_of(j * rows, rows), rows)

    greet([(None, (dp, lax.rem(me + k, groups))) for k in range(1, groups)])
    own = pltpu.make_async_copy(attn_ref, heads_buf.at[me], local_sem)
    own.start()

    def attn_copy(k, i):
        peer = lax.rem(me + k, groups)
        at = span(lax.rem(peer + 1 + i, groups))
        return pltpu.make_async_remote_copy(
            attn_ref.at[at], heads_buf.at[me, at], attn_send.at[k, i], attn_recv.at[k, i],
            device_id=(dp, peer), device_id_type=MESH,
        )

    def part_copy(i):
        peer = lax.rem(me + 1 + i, groups)
        return pltpu.make_async_remote_copy(
            part_out.at[i], part_in.at[i], part_send.at[i], part_recv.at[i],
            device_id=(dp, peer), device_id_type=MESH,
        )

    def out_copy(k):
        peer = lax.rem(me + k, groups)
        return pltpu.make_async_remote_copy(
            result, out_ref.at[span(me)], out_send.at[k], out_recv.at[k],
            device_id=(dp, peer), device_id_type=MESH,
        )

    for i in range(groups):
        for k in range(1, groups):
            attn_copy(k, i).start()
    for t in range(groups):
        wout[:, t * width : (t + 1) * width] = wout_ref[t]
    own.wait()
    for i in range(groups):
        for k in range(1, groups):
            attn_copy(k, i).wait_recv()
        at = span(lax.rem(me + 1 + i, groups))
        attn = jnp.concatenate([heads_buf[t, at, :] for t in range(groups)], axis=1)
        proj = lax.dot_general(
            attn, wout[...], (((1,), (1,)), ((), ())), preferred_element_type=F32
        )
        first = norm(tok_ref[at, :].astype(F32) + proj).astype(BF)
        hidden = jnp.dot(first, ffw_ref[:, :ff], preferred_element_type=F32)
        inner = (0.5 * hidden * (1.0 + lax.erf(hidden * 0.7071067811865476))).astype(BF)
        part = lax.dot_general(
            inner, ffw_ref[:, ff:], (((1,), (1,)), ((), ())), preferred_element_type=F32
        )
        if i < groups - 1:
            part_out[i] = part.astype(BF)
            part_copy(i).start()
        else:
            total = part
            for n in range(groups - 1):
                part_copy(n).wait_recv()
                total = total + part_in[n].astype(F32)
            value = norm(first.astype(F32) + total) * live_ref[at, :]
            result[...] = value.astype(BF)
    final = pltpu.make_async_copy(result, out_ref.at[span(me)], local_sem)
    final.start()
    for k in range(1, groups):
        out_copy(k).start()
    for k in range(1, groups):
        out_copy(k).wait()
        for i in range(groups):
            attn_copy(k, i).wait_send()
    for n in range(groups - 1):
        part_copy(n).wait_send()
    final.wait()


def tail(attn, tokens, ffw, wout, live, groups, cid):
    rows, width = attn.shape
    wide = tokens.shape[1]
    share = rows // groups
    vmem = pl.BlockSpec(memory_space=pltpu.VMEM)
    return pl.pallas_call(
        functools.partial(tail_kernel, groups),
        out_shape=jax.ShapeDtypeStruct(tokens.shape, BF),
        in_specs=[vmem] * 5,
        out_specs=pl.BlockSpec(memory_space=pl.ANY),
        scratch_shapes=[
            pltpu.VMEM((groups, rows, width), BF),
            pltpu.VMEM((wide, wide), BF),
            pltpu.VMEM((groups - 1, share, wide), BF),
            pltpu.VMEM((groups - 1, share, wide), BF),
            pltpu.VMEM((share, wide), BF),
            pltpu.SemaphoreType.DMA((groups, groups)),
            pltpu.SemaphoreType.DMA((groups, groups)),
            pltpu.SemaphoreType.DMA((groups,)),
            pltpu.SemaphoreType.DMA((groups,)),
            pltpu.SemaphoreType.DMA((groups,)),
            pltpu.SemaphoreType.DMA((groups,)),
            pltpu.SemaphoreType.DMA,
        ],
        compiler_params=pltpu.CompilerParams(
            collective_id=cid, has_side_effects=True, vmem_limit_bytes=48 * 2**20
        ),
        name="tail",
    )(attn, tokens, ffw, wout, live)


def shards(tokens, w_qkv, w_out, w_up, w_down, slot_request):
    groups = lax.axis_size("tensor")
    dp = lax.axis_index("dp")
    slab, wide = w_qkv.shape[0], tokens.shape[1]
    heads = wide // HEAD // groups
    width = heads * HEAD
    rows = tokens.shape[0]

    qkv_w = w_qkv.astype(BF).reshape(slab, groups, heads, 3, HEAD)
    qkv_w = jnp.transpose(qkv_w, (1, 0, 3, 2, 4)).reshape(groups, slab, 3 * width)
    up_w = jnp.transpose(w_up.astype(BF).reshape(slab, groups, -1), (1, 0, 2))
    down_w = jnp.transpose(w_down.astype(BF).reshape(groups, -1, slab), (0, 2, 1))
    ffw = jnp.concatenate([up_w, down_w], axis=2)
    out_w = jnp.transpose(w_out.astype(BF).reshape(groups, width, slab), (0, 2, 1))
    mine = exchange([qkv_w, out_w, ffw], groups, 0)
    mine = [x.reshape(groups * slab, x.shape[2]) for x in mine]
    qkv_block, out_block = gather_dp(mine[:2], 1)
    late, qkv_block = lax.optimization_barrier((mine[2], qkv_block))
    ffw = lax.all_gather(late, "dp", axis=0, tiled=True)
    qkv = jnp.dot(
        tokens, qkv_block.reshape(wide, 3 * width), preferred_element_type=F32
    ).astype(BF)
    kv, wout = gather_dp(
        [qkv], 2, cols=(width, 3 * width), side=out_block.reshape(wide, width), groups=groups
    )
    kv = kv.reshape(-1, 2 * width)
    attn = attend(qkv, kv, slot_request, dp)
    own_ids = lax.dynamic_slice_in_dim(slot_request.reshape(-1), dp * rows, rows, 0)
    live = (own_ids >= 0).astype(F32)[:, None]
    return tail(attn, tokens, ffw, wout, live, groups, 3)


def solution(mesh):
    in_specs = (
        P("dp", None),
        P(("dp", "tensor"), None),
        P(None, ("dp", "tensor")),
        P(("dp", "tensor"), None),
        P(None, ("dp", "tensor")),
        P(),
    )
    out_specs = P("dp", None)
    return jax.shard_map(shards, mesh=mesh, in_specs=in_specs, out_specs=out_specs, check_vma=False)
```

```python
import functools

import jax
import jax.numpy as jnp
from jax import lax
from jax.experimental import pallas as pl
from jax.experimental.pallas import tpu as pltpu
from jax.sharding import PartitionSpec as P

HEAD = 64
MESH = pl.DeviceIdType.MESH
GROUP = 4
BF = jnp.bfloat16
F32 = jnp.float32


def greet(targets):
    barrier = pltpu.get_barrier_semaphore()
    for cond, dev in targets:
        if cond is None:
            pl.semaphore_signal(barrier, inc=1, device_id=dev, device_id_type=MESH)
        else:

            @pl.when(cond)
            def _(dev=dev):
                pl.semaphore_signal(barrier, inc=1, device_id=dev, device_id_type=MESH)

    count = sum(1 if cond is None else jnp.where(cond, 1, 0) for cond, _ in targets)
    pl.semaphore_wait(barrier, count)


def gather_kernel(chips, count, cols, groups, *refs):
    total = count + (1 if groups else 0)
    x_refs, out_refs = list(refs[:total]), refs[total : 2 * total]
    gather_body(chips, count, cols, groups, x_refs, out_refs, refs[2 * total :], True)


def front_kernel(chips, groups, count, every, *refs):
    x_refs, full_refs = refs[:every], refs[every : every + count]
    late_refs, refs = refs[every + count : 2 * every], refs[2 * every :]
    held, send_sem, recv_sem, own_sem = refs[:count], refs[count], refs[count + 1], refs[count + 2]
    dp = lax.axis_index("dp")
    me = lax.axis_index("tensor")
    landing = list(held) + list(late_refs)

    def swap(n, k):
        peer = lax.rem(me + k, groups)
        return pltpu.make_async_remote_copy(
            x_refs[n].at[peer], landing[n].at[me], send_sem.at[n, k], recv_sem.at[n, k],
            device_id=(dp, peer), device_id_type=MESH,
        )

    def keep(n):
        return pltpu.make_async_copy(x_refs[n].at[me], landing[n].at[me], own_sem.at[n])

    def begin():
        for n in range(every):
            for k in range(1, groups):
                swap(n, k).start()
            keep(n).start()
        for n in range(count):
            for k in range(1, groups):
                swap(n, k).wait()
            keep(n).wait()

    gather_body(chips, count, None, groups, held, full_refs, refs[count + 3 :], False, begin)
    for n in range(count, every):
        for k in range(1, groups):
            swap(n, k).wait()
        keep(n).wait()


def front(arrays, count, groups, cid):
    dps = lax.axis_size("dp")
    chips = dps // 2
    every = len(arrays)
    hbm = pl.BlockSpec(memory_space=pl.ANY)
    return pl.pallas_call(
        functools.partial(front_kernel, chips, groups, count, every),
        out_shape=[jax.ShapeDtypeStruct((dps,) + x.shape, BF) for x in arrays[:count]]
        + [jax.ShapeDtypeStruct(x.shape, BF) for x in arrays[count:]],
        in_specs=[hbm] * every,
        out_specs=[hbm] * every,
        scratch_shapes=[pltpu.VMEM(x.shape, BF) for x in arrays[:count]]
        + [
            pltpu.SemaphoreType.DMA((every, groups)),
            pltpu.SemaphoreType.DMA((every, groups)),
            pltpu.SemaphoreType.DMA((every,)),
            pltpu.SemaphoreType.DMA((count, chips)),
            pltpu.SemaphoreType.DMA((count, chips)),
            pltpu.SemaphoreType.DMA((count, chips)),
            pltpu.SemaphoreType.DMA((count, dps)),
            pltpu.SemaphoreType.DMA((count + 1,)),
            pltpu.SemaphoreType.DMA((groups,)),
            pltpu.SemaphoreType.DMA((groups,)),
        ],
        compiler_params=pltpu.CompilerParams(collective_id=cid, has_side_effects=True),
        name="front",
    )(*arrays)


def gather_body(chips, count, cols, groups, x_refs, out_refs, sems, with_side, begin=None):
    right_sem, left_sem, core_sem, recv_sem, local_sem, side_send, side_recv = sems
    dp = lax.axis_index("dp")
    tensor = lax.axis_index("tensor")
    chip, core = dp // 2, lax.rem(dp, 2)
    other = 1 - core
    partner = (2 * chip + other, tensor)
    has_right, has_left = chip + 1 < chips, chip > 0
    right = (2 * jnp.minimum(chip + 1, chips - 1) + core, tensor)
    left = (2 * jnp.maximum(chip - 1, 0) + core, tensor)
    peers = [(dp, lax.rem(tensor + k, groups)) for k in range(1, groups)] if groups else []
    greet(
        [(None, partner), (has_right, right), (has_left, left)]
        + [(None, peer) for peer in peers]
    )
    if cols is not None:
        x_refs[0] = x_refs[0].at[:, cols[0] : cols[1]]
    if begin is not None:
        begin()

    def copy_of(n, source, block, send, device):
        return pltpu.make_async_remote_copy(
            source, out_refs[n].at[block], send, recv_sem.at[n, block],
            device_id=device, device_id_type=MESH,
        )

    for n in range(count):

        @pl.when(has_right)
        def _(n=n):
            copy_of(n, x_refs[n], dp, right_sem.at[n, 0], right).start()

        @pl.when(has_left)
        def _(n=n):
            copy_of(n, x_refs[n], dp, left_sem.at[n, 0], left).start()

        copy_of(n, x_refs[n], dp, core_sem.at[n, chip], partner).start()
    for n in range(count):
        pltpu.make_async_copy(x_refs[n], out_refs[n].at[dp], local_sem.at[n]).start()
    side = []
    for k, peer in enumerate(peers if with_side else []):
        side.append(
            pltpu.make_async_remote_copy(
                x_refs[count], out_refs[count].at[tensor], side_send.at[k], side_recv.at[k],
                device_id=peer, device_id_type=MESH,
            )
        )
    if with_side:
        side.append(
            pltpu.make_async_copy(
                x_refs[count], out_refs[count].at[tensor], local_sem.at[count]
            )
        )
    for copy in side:
        copy.start()
    for s in range(1, chips):
        for n in range(count):
            for away, has_next, sems, following in (
                (chip - s, has_right, right_sem, right),
                (chip + s, has_left, left_sem, left),
            ):

                @pl.when(jnp.logical_and(away >= 0, away < chips))
                def _(n=n, away=away, has_next=has_next, sems=sems, following=following, s=s):
                    block = 2 * away + core
                    here = out_refs[n].at[block]
                    copy_of(n, here, block, core_sem.at[n, away], partner).wait_recv()

                    @pl.when(has_next)
                    def _():
                        copy_of(n, here, block, sems.at[n, s], following).start()

                    copy_of(n, here, block, core_sem.at[n, away], partner).start()

    for n in range(count):
        for away in range(chips):
            block = 2 * away + other
            copy_of(n, x_refs[n], block, core_sem.at[n, away], partner).wait()
        for s in range(chips):

            @pl.when(jnp.logical_and(has_right, chip - s >= 0))
            def _(n=n, s=s):
                copy_of(n, x_refs[n], dp, right_sem.at[n, s], right).wait_send()

            @pl.when(jnp.logical_and(has_left, chip + s < chips))
            def _(n=n, s=s):
                copy_of(n, x_refs[n], dp, left_sem.at[n, s], left).wait_send()

        pltpu.make_async_copy(x_refs[n], out_refs[n].at[dp], local_sem.at[n]).wait()
    for copy in side:
        copy.wait()


def gather_dp(arrays, cid, cols=None, side=None, groups=0):
    n = lax.axis_size("dp")
    chips = n // 2
    count = len(arrays)
    shapes = [x.shape for x in arrays]
    if cols is not None:
        shapes[0] = (shapes[0][0], cols[1] - cols[0])
    shapes = [(n,) + shape for shape in shapes]
    if side is not None:
        arrays = arrays + [side]
        shapes.append((groups,) + side.shape)
    hbm = pl.BlockSpec(memory_space=pl.ANY)
    return pl.pallas_call(
        functools.partial(gather_kernel, chips, count, cols, groups),
        out_shape=[jax.ShapeDtypeStruct(shape, BF) for shape in shapes],
        in_specs=[hbm] * len(shapes),
        out_specs=[hbm] * len(shapes),
        scratch_shapes=[
            pltpu.SemaphoreType.DMA((count, chips)),
            pltpu.SemaphoreType.DMA((count, chips)),
            pltpu.SemaphoreType.DMA((count, chips)),
            pltpu.SemaphoreType.DMA((count, n)),
            pltpu.SemaphoreType.DMA((count + 1,)),
            pltpu.SemaphoreType.DMA((max(groups, 1),)),
            pltpu.SemaphoreType.DMA((max(groups, 1),)),
        ],
        compiler_params=pltpu.CompilerParams(collective_id=cid, has_side_effects=True),
        cost_estimate=pl.CostEstimate(
            flops=0, bytes_accessed=n * arrays[0].size * 4, transcendentals=0
        ),
        name="gather_dp",
    )(*arrays)


def attend_kernel(heads, page, pages_ref, count_ref, q_ref, kv_ref, qid_ref, kid_ref, out_ref, qbd):
    width = heads * HEAD
    pair = 2 * HEAD
    step = pl.program_id(0)
    low = lax.broadcasted_iota(jnp.int32, (page, pair), 1) < HEAD
    q = q_ref[...] * jnp.asarray(0.125, BF)
    zero = jnp.zeros((page, pair), BF)
    for h in range(heads // 2):
        both = q[:, h * pair : (h + 1) * pair]
        qbd[h, :page, :] = jnp.where(low, both, zero)
        qbd[h, page:, :] = jnp.where(low, zero, both)
    own = jnp.concatenate([qid_ref[...]] * 2, axis=0)
    rows = 2 * page
    count = count_ref[step]

    def body(i, carry):
        blocks, ids = [], []
        for g in range(GROUP):
            at = i * GROUP + g
            p = pages_ref[step, at]
            blocks.append(kv_ref[pl.ds(pl.multiple_of(p * page, page), page), :])
            ids.append(jnp.where(at < count, kid_ref[pl.ds(p, 1), :], -2))
        block = jnp.concatenate(blocks, axis=0)
        kid = jnp.concatenate(ids, axis=1)
        allowed = own == kid
        after = []
        scores = [
            lax.dot_general(
                qbd[h], block[:, h * pair : (h + 1) * pair],
                (((1,), (1,)), ((), ())), preferred_element_type=F32,
            )
            for h in range(heads // 2)
        ]
        for h in range(heads // 2):
            top, total, acc = carry[h]
            value = block[:, width + h * pair : width + (h + 1) * pair]
            s = jnp.where(allowed, scores[h], -1e30)
            new_top = jnp.maximum(top, jnp.max(s, axis=1, keepdims=True))
            w = jnp.exp(s - new_top)
            alpha = jnp.exp(top - new_top)
            total = total * alpha + jnp.sum(w, axis=1, keepdims=True)
            acc = acc * alpha + jnp.dot(w.astype(BF), value, preferred_element_type=F32)
            after.append((new_top, total, acc))
        return tuple(after)

    init = (
        jnp.full((rows, 1), -1e29, F32),
        jnp.zeros((rows, 1), F32),
        jnp.zeros((rows, pair), F32),
    )
    final = lax.fori_loop(0, (count + GROUP - 1) // GROUP, body, (init,) * (heads // 2))
    for h in range(heads // 2):
        _, total, acc = final[h]
        acc = (acc / total).astype(BF)
        out_ref[:, h * pair : (h + 1) * pair] = jnp.where(low, acc[:page], acc[page:])


def attend(q, kv, slots, dp):
    rows, width = q.shape[0], kv.shape[1] // 2
    total_pages, page = slots.shape
    heads = width // HEAD
    own_pages = rows // page
    requests = jnp.arange(-1, 4, dtype=jnp.int32)
    holds = jnp.any(slots[:, :, None] == requests[None, None, :], axis=1)
    own_holds = lax.dynamic_slice_in_dim(holds, dp * own_pages, own_pages, 0)
    need = jnp.any(own_holds[:, None, :] & holds[None, :, :], axis=-1)
    need_int = need.astype(jnp.int32)
    index = jnp.arange(total_pages, dtype=jnp.int32)
    before = (index[:, None] > index[None, :]).astype(jnp.int32)
    place = jnp.sum(need_int[:, None, :] * before[None], axis=-1)
    hit = need[:, :, None] & (place[:, :, None] == index[None, None, :])
    lists = jnp.sum(jnp.where(hit, index[None, :, None], 0), axis=1).astype(jnp.int32)
    lists = jnp.pad(lists, ((0, 0), (0, GROUP)))
    counts = jnp.sum(need_int, axis=1).astype(jnp.int32)
    own_ids = lax.dynamic_slice_in_dim(slots.reshape(-1), dp * rows, rows, 0)[:, None]
    return pl.pallas_call(
        functools.partial(attend_kernel, heads, page),
        out_shape=jax.ShapeDtypeStruct((rows, width), BF),
        grid_spec=pltpu.PrefetchScalarGridSpec(
            num_scalar_prefetch=2,
            grid=(own_pages,),
            in_specs=[
                pl.BlockSpec((page, width), lambda i, *_: (i, 0)),
                pl.BlockSpec(kv.shape, lambda i, *_: (0, 0)),
                pl.BlockSpec((page, 1), lambda i, *_: (i, 0)),
                pl.BlockSpec(slots.shape, lambda i, *_: (0, 0)),
            ],
            out_specs=pl.BlockSpec((page, width), lambda i, *_: (i, 0)),
            scratch_shapes=[pltpu.VMEM((heads // 2, 2 * page, 2 * HEAD), BF)],
        ),
        compiler_params=pltpu.CompilerParams(vmem_limit_bytes=40 * 2**20),
        cost_estimate=pl.CostEstimate(
            flops=rows * kv.shape[0] * 256 * 4 * 2, bytes_accessed=2 * kv.size,
            transcendentals=rows * kv.shape[0] * heads // 2,
        ),
        name="attend",
    )(lists, counts, q, kv, own_ids, slots)


def norm(value):
    mean = jnp.mean(value, axis=-1, keepdims=True)
    centred = value - mean
    spread = jnp.mean(centred * centred, axis=-1, keepdims=True)
    return centred * lax.rsqrt(spread + 1e-05)


def tail_kernel(
    groups, attn_ref, tok_ref, up_ref, down_ref, wout_ref, live_ref, out_ref,
    heads_buf, wout, part_out, part_in, result,
    attn_send, attn_recv, part_send, part_recv, out_send, out_recv, local_sem,
):
    dp = lax.axis_index("dp")
    me = lax.axis_index("tensor")
    rows = attn_ref.shape[0] // groups
    width = attn_ref.shape[1]

    def span(j):
        return pl.ds(pl.multiple_of(j * rows, rows), rows)

    greet([(None, (dp, lax.rem(me + k, groups))) for k in range(1, groups)])
    own = pltpu.make_async_copy(attn_ref, heads_buf.at[me], local_sem)
    own.start()

    def attn_copy(k, i):
        peer = lax.rem(me + k, groups)
        at = span(lax.rem(peer + 1 + i, groups))
        return pltpu.make_async_remote_copy(
            attn_ref.at[at], heads_buf.at[me, at], attn_send.at[k, i], attn_recv.at[k, i],
            device_id=(dp, peer), device_id_type=MESH,
        )

    def part_copy(i):
        peer = lax.rem(me + 1 + i, groups)
        return pltpu.make_async_remote_copy(
            part_out.at[i], part_in.at[i], part_send.at[i], part_recv.at[i],
            device_id=(dp, peer), device_id_type=MESH,
        )

    def out_copy(k):
        peer = lax.rem(me + k, groups)
        return pltpu.make_async_remote_copy(
            result, out_ref.at[span(me)], out_send.at[k], out_recv.at[k],
            device_id=(dp, peer), device_id_type=MESH,
        )

    for i in range(groups):
        for k in range(1, groups):
            attn_copy(k, i).start()
    for t in range(groups):
        wout[:, t * width : (t + 1) * width] = wout_ref[t]
    own.wait()
    for i in range(groups):
        for k in range(1, groups):
            attn_copy(k, i).wait_recv()
        at = span(lax.rem(me + 1 + i, groups))
        attn = jnp.concatenate([heads_buf[t, at, :] for t in range(groups)], axis=1)
        proj = lax.dot_general(
            attn, wout[...], (((1,), (1,)), ((), ())), preferred_element_type=F32
        )
        first = norm(tok_ref[at, :].astype(F32) + proj).astype(BF)
        hidden = jnp.dot(first, up_ref[...], preferred_element_type=F32)
        inner = (0.5 * hidden * (1.0 + lax.erf(hidden * 0.7071067811865476))).astype(BF)
        part = lax.dot_general(
            inner, down_ref[...], (((1,), (1,)), ((), ())), preferred_element_type=F32
        )
        if i < groups - 1:
            part_out[i] = part.astype(BF)
            part_copy(i).start()
        else:
            total = part
            for n in range(groups - 1):
                part_copy(n).wait_recv()
                total = total + part_in[n].astype(F32)
            value = norm(first.astype(F32) + total) * live_ref[at, :]
            result[...] = value.astype(BF)
    final = pltpu.make_async_copy(result, out_ref.at[span(me)], local_sem)
    final.start()
    for k in range(1, groups):
        out_copy(k).start()
    for k in range(1, groups):
        out_copy(k).wait()
        for i in range(groups):
            attn_copy(k, i).wait_send()
    for n in range(groups - 1):
        part_copy(n).wait_send()
    final.wait()


def tail(attn, tokens, up, down, wout, live, groups, cid):
    rows, width = attn.shape
    wide = tokens.shape[1]
    share = rows // groups
    vmem = pl.BlockSpec(memory_space=pltpu.VMEM)
    return pl.pallas_call(
        functools.partial(tail_kernel, groups),
        out_shape=jax.ShapeDtypeStruct(tokens.shape, BF),
        in_specs=[vmem] * 6,
        out_specs=pl.BlockSpec(memory_space=pl.ANY),
        scratch_shapes=[
            pltpu.VMEM((groups, rows, width), BF),
            pltpu.VMEM((wide, wide), BF),
            pltpu.VMEM((groups - 1, share, wide), BF),
            pltpu.VMEM((groups - 1, share, wide), BF),
            pltpu.VMEM((share, wide), BF),
            pltpu.SemaphoreType.DMA((groups, groups)),
            pltpu.SemaphoreType.DMA((groups, groups)),
            pltpu.SemaphoreType.DMA((groups,)),
            pltpu.SemaphoreType.DMA((groups,)),
            pltpu.SemaphoreType.DMA((groups,)),
            pltpu.SemaphoreType.DMA((groups,)),
            pltpu.SemaphoreType.DMA,
        ],
        compiler_params=pltpu.CompilerParams(
            collective_id=cid, has_side_effects=True, vmem_limit_bytes=48 * 2**20
        ),
        name="tail",
    )(attn, tokens, up, down, wout, live)


def shards(tokens, w_qkv, w_out, w_up, w_down, slot_request):
    groups = lax.axis_size("tensor")
    dp = lax.axis_index("dp")
    slab, wide = w_qkv.shape[0], tokens.shape[1]
    heads = wide // HEAD // groups
    width = heads * HEAD
    rows = tokens.shape[0]

    qkv_w = w_qkv.astype(BF).reshape(slab, groups, heads, 3, HEAD)
    qkv_w = jnp.transpose(qkv_w, (1, 0, 3, 2, 4)).reshape(groups, slab, 3 * width)
    up_w = jnp.transpose(w_up.astype(BF).reshape(slab, groups, -1), (1, 0, 2))
    down_w = jnp.transpose(w_down.astype(BF).reshape(groups, -1, slab), (0, 2, 1))
    out_w = jnp.transpose(w_out.astype(BF).reshape(groups, width, slab), (0, 2, 1))
    qkv_block, out_block, up_part, down_part = front([qkv_w, out_w, up_w, down_w], 2, groups, 0)
    up = lax.all_gather(up_part.reshape(groups * slab, -1), "dp", axis=0, tiled=True)
    qkv = jnp.dot(
        tokens, qkv_block.reshape(wide, 3 * width), preferred_element_type=F32
    ).astype(BF)
    kv, wout = gather_dp(
        [qkv], 2, cols=(width, 3 * width), side=out_block.reshape(wide, width), groups=groups
    )
    down_part, up, kv = lax.optimization_barrier((down_part, up, kv))
    down = lax.all_gather(down_part.reshape(groups * slab, -1), "dp", axis=0, tiled=True)
    kv = kv.reshape(-1, 2 * width)
    attn = attend(qkv, kv, slot_request, dp)
    own_ids = lax.dynamic_slice_in_dim(slot_request.reshape(-1), dp * rows, rows, 0)
    live = (own_ids >= 0).astype(F32)[:, None]
    return tail(attn, tokens, up, down, wout, live, groups, 3)


def solution(mesh):
    in_specs = (
        P("dp", None),
        P(("dp", "tensor"), None),
        P(None, ("dp", "tensor")),
        P(("dp", "tensor"), None),
        P(None, ("dp", "tensor")),
        P(),
    )
    out_specs = P("dp", None)
    return jax.shard_map(shards, mesh=mesh, in_specs=in_specs, out_specs=out_specs, check_vma=False)
```
